512 devices in a mesh: expert: 32 (over y, x, z_hi), tensor: 16 (over z_lo, core).
Axes of the slice: x: 4, y: 4, z: 16 (z_hi: 2, z_lo: 8; z = z_hi * 8 + z_lo), core: 2. Of those that a mesh axis runs over, the one named last changes fastest.
Arguments:
- tokens: bfloat16 [4096, 2560], P('expert', 'tensor'), may hold values from -6 to 6
- first_gain: float32 [2560], replicated, may hold values from 0.1 to 1.9
- dense_gate: bfloat16 [2560, 8192], P('expert', 'tensor'), may hold values from -0.125 to 0.125
- dense_up: bfloat16 [2560, 8192], P('expert', 'tensor'), may hold values from -0.125 to 0.125
- dense_down: bfloat16 [2560, 8192], P('expert', 'tensor'), may hold values from -0.0625 to 0.0625
- second_gain: float32 [2560], replicated, may hold values from 0.1 to 1.9
- shared_gate: bfloat16 [2560, 4096], P('expert', 'tensor'), may hold values from -0.125 to 0.125
- shared_up: bfloat16 [2560, 4096], P('expert', 'tensor'), may hold values from -0.125 to 0.125
- shared_down: bfloat16 [2560, 4096], P('expert', 'tensor'), may hold values from -0.09375 to 0.09375
- expert_gate: bfloat16 [32, 2560, 4096], P('expert', None, 'tensor'), may hold values from -0.125 to 0.125
- expert_up: bfloat16 [32, 2560, 4096], P('expert', None, 'tensor'), may hold values from -0.125 to 0.125
- expert_down: bfloat16 [32, 2560, 4096], P('expert', None, 'tensor'), may hold values from -0.09375 to 0.09375
- routes: int32 [4096, 1], P('expert'), may hold values from 0 to 31; in each aligned block of 128 rows (0 to 127, 128 to 255, ...) at most 8 rows name the same one
- route_gate: float32 [4096, 1], P('expert'), may hold values from 0.25 to 1
Outputs:
- mixed: bfloat16 [4096, 2560], P('expert', 'tensor')
The draws below stay inside these ranges and needn't reach their ends.
Inputs may be any that keep to these rules, and one draw needn't show every extreme that they name: `routes`: within each aligned block of 128 tokens (the tokens of one index of expert), no expert is named by more than 8 tokens, and that number is reached in some block.
All inputs are finite; a program needn't handle non-finite values.
Results may differ from the reference program's by a relative error of at most 0.025.
Values may be sent and summed in bfloat16 or wider, within the bound.
A program may use at most 64 MiB of HBM per device.

```python
import math
import jax
import jax.numpy as jnp
import numpy as np
from jax import lax

D = 2560
FFD = 8192
HE = 4096
HS = 4096
TOK_DEV = 128
TOKENS = 4096
EXPERTS = 32
DEPTH = 8
CAPACITY = 256
N_EXPERT = 32
N_TENSOR = 16


def levels(rng, shape, split, low, top_value):
    def one(position, parts):
        heights = jax.random.uniform(jax.random.fold_in(jax.random.fold_in(rng, 6), position), (parts,), jnp.float32, low / len(split), top_value / len(split))
        return jnp.repeat(jnp.exp(heights), shape[position] // parts).reshape((-1,) + (1,) * (len(shape) - position - 1))

    level = one(*split[0])
    for cut in split[1:]:
        level = level * one(*cut)
    return level


def assign_block(stream_key, own, number, rows, number_of, top, bound, lean):
    ranking = jax.random.permutation(stream_key, number_of)
    heavy_load, ordinary = portions_of(number_of, rows * top, bound, lean, True), portions_of(number_of, rows * top, bound, lean, False)
    places = jnp.arange(number_of)

    def named(lengths, rotation):
        used = int((lengths > 0).sum())
        fixed = max(1, used // 4)
        passed = fixed + (places - fixed + rotation * (used - fixed)) % max(1, number_of - fixed)
        return jnp.zeros((number_of,), jnp.int32).at[ranking[jnp.where(places < fixed, places, passed)]].set(jnp.asarray(lengths, jnp.int32))

    lengths = jnp.where(number % 4 == 0, named(heavy_load, number // 4), named(ordinary, number - number // 4 - 1))
    mixed = jax.random.permutation(jax.random.fold_in(own, 3), number_of)
    donor, sink = mixed[0:number_of // 2 * 2:2], mixed[1:number_of // 2 * 2:2]
    margin = jnp.minimum(lengths[donor] - 1, bound - lengths[sink]) // 2
    margin = jnp.where((donor == ranking[0]) | (sink == ranking[0]) | (lengths[sink] == 0), 0, jnp.maximum(margin, 0))
    passed = jax.random.randint(jax.random.fold_in(own, 4), (number_of // 2,), 0, 1 << 20) % (margin + 1)
    lengths = lengths.at[donor].add(-passed).at[sink].add(passed)
    items = jnp.searchsorted(jnp.cumsum(lengths), jnp.arange(rows * top), side="right").astype(jnp.int32)
    table = items.reshape(top, rows).T
    table = table[jax.random.permutation(jax.random.fold_in(own, 1), rows)]
    rotation = jax.random.randint(jax.random.fold_in(own, 2), (rows, 1), 0, top)
    return jnp.take_along_axis(table, (jnp.arange(top)[None, :] + rotation) % top, axis=1)


def portions_of(number_of, total, limit, slope, full):
    portions = [(1 << 20) // math.isqrt(rank ** slope) + 1 for rank in range(1, number_of + 1)]
    largest = limit if full else min(limit, max(-(-total // number_of), total * portions[0] // sum(portions)))
    least = 1 if total - largest >= number_of - 1 else 0
    holding, surplus = [largest] + [least] * (number_of - 1), total - largest - least * (number_of - 1)
    while surplus > 0:
        free = [i for i in range(1, number_of) if holding[i] < largest] or [i for i in range(1, number_of) if holding[i] < limit]
        whole, left = sum([portions[i] for i in free]), surplus
        for i in free:
            more = min(limit - holding[i], max(1, left * portions[i] // whole), surplus)
            holding[i] = holding[i] + more
            surplus = surplus - more
    return np.array(holding)


def gaussian(key, shape, deviation, reach, shards=(), kind=jnp.bfloat16):
    level = levels(key, shape, shards, -0.22, 0.18) if shards else 1.0
    result = jax.random.normal(key, shape, jnp.float32) * deviation * level
    return jnp.minimum(jnp.maximum(result, -reach), reach).astype(kind)


def setup_inputs(seed: int = 0) -> dict:
    streams_of = jax.random.split(jax.random.key(seed), 15)
    tokens = gaussian(streams_of[0], (TOKENS, D), 1.0, 6.0, ((0, 32), (1, 16)))
    first_gain = jnp.clip(1.0 + 0.18 * jax.random.normal(streams_of[1], (D,), jnp.float32), 0.1, 1.9)
    dense_gate = gaussian(streams_of[2], (D, FFD), D ** -0.5, 0.125, ((0, 32), (1, 16)))
    dense_up = gaussian(streams_of[3], (D, FFD), D ** -0.5, 0.125, ((0, 32), (1, 16)))
    dense_down = gaussian(streams_of[4], (D, FFD), FFD ** -0.5, 0.0625, ((0, 32), (1, 16)))
    second_gain = jnp.clip(1.0 + 0.18 * jax.random.normal(streams_of[5], (D,), jnp.float32), 0.1, 1.9)
    shared_gate = gaussian(streams_of[6], (D, HS), D ** -0.5, 0.125, ((0, 32), (1, 16)))
    shared_up = gaussian(streams_of[7], (D, HS), D ** -0.5, 0.125, ((0, 32), (1, 16)))
    shared_down = gaussian(streams_of[8], (D, HS), HS ** -0.5, 0.09375, ((0, 32), (1, 16)))
    expert_gate = gaussian(streams_of[9], (EXPERTS, D, HE), D ** -0.5, 0.125, ((0, 32), (2, 16)))
    expert_up = gaussian(streams_of[10], (EXPERTS, D, HE), D ** -0.5, 0.125, ((0, 32), (2, 16)))
    expert_down = gaussian(streams_of[11], (EXPERTS, D, HE), HE ** -0.5, 0.09375, ((0, 32), (2, 16)))
    routes_keys = jax.random.split(jax.random.fold_in(streams_of[12], 1), TOKENS // TOK_DEV)
    routes_turns = jax.random.permutation(jax.random.fold_in(streams_of[12], 3), TOKENS // TOK_DEV)
    routes = jax.vmap(lambda own, number: assign_block(jax.random.fold_in(streams_of[12], 2), own, number, TOK_DEV, EXPERTS, 1, DEPTH, 2))(routes_keys, routes_turns).reshape((TOKENS, 1))
    route_gate = jnp.clip(0.25 + 0.75 * jax.random.uniform(streams_of[13], (TOKENS, 1), jnp.float32) ** levels(streams_of[13], (TOKENS, 1), ((0, 32),), -0.2, 0.2), 0.25, 1.0)
    return {"tokens": tokens, "first_gain": first_gain, "dense_gate": dense_gate, "dense_up": dense_up, "dense_down": dense_down, "second_gain": second_gain, "shared_gate": shared_gate, "shared_up": shared_up, "shared_down": shared_down, "expert_gate": expert_gate, "expert_up": expert_up, "expert_down": expert_down, "routes": routes, "route_gate": route_gate}


EPSILON = 1e-05

def rms_scaled(rows, gain):
    wide_rows = rows.astype(jnp.float32)
    square_mean = lax.optimization_barrier(jnp.mean(wide_rows * wide_rows, axis=1, keepdims=True))
    return (wide_rows * lax.rsqrt(square_mean + EPSILON) * gain.astype(jnp.float32)).astype(jnp.bfloat16)

def gated_hidden(normed, gate_weight, up_weight):
    gate_part = jnp.dot(normed, gate_weight, preferred_element_type=jnp.float32)
    up_part = jnp.dot(normed, up_weight, preferred_element_type=jnp.float32)
    return (jax.nn.silu(gate_part) * up_part).astype(jnp.bfloat16)

def rounded(values):
    narrow = values.astype(jnp.bfloat16)
    narrow = lax.optimization_barrier(narrow)
    return narrow.astype(jnp.float32)

def reference(tokens, first_gain, dense_gate, dense_up, dense_down, second_gain, shared_gate, shared_up, shared_down, expert_gate, expert_up, expert_down, routes, route_gate):
    first_normed = rms_scaled(tokens, first_gain)
    dense_hidden = gated_hidden(first_normed, dense_gate, dense_up)
    dense_block = FFD // N_TENSOR

    def dense_add(summed, block_index):
        hidden_block = lax.dynamic_slice_in_dim(dense_hidden, block_index * dense_block, dense_block, 1)
        down_block = lax.dynamic_slice_in_dim(dense_down, block_index * dense_block, dense_block, 1)
        product = lax.dot_general(hidden_block, down_block, (((1,), (1,)), ((), ())), preferred_element_type=jnp.float32)
        return (summed + rounded(product), None)
    dense_sum, _ = lax.scan(dense_add, jnp.zeros((TOKENS, D), jnp.float32), jnp.arange(N_TENSOR, dtype=jnp.int32))
    middle = (tokens.astype(jnp.float32) + dense_sum).astype(jnp.bfloat16)
    second_normed = rms_scaled(middle, second_gain)
    expert_id = routes[:, 0].astype(jnp.int32)
    blocks = expert_id.reshape(N_EXPERT, TOK_DEV)
    matches = (blocks[:, :, None] == jnp.arange(EXPERTS, dtype=jnp.int32)[None, None, :]).astype(jnp.int32)
    earlier = jnp.cumsum(matches, axis=1) - matches
    slot_rank = lax.optimization_barrier(jnp.sum(earlier * matches, axis=2))
    slot = (jnp.arange(N_EXPERT, dtype=jnp.int32)[:, None] * DEPTH + slot_rank).reshape(TOKENS).astype(jnp.int32)
    packed = jnp.zeros((EXPERTS, CAPACITY, D), jnp.bfloat16).at[expert_id, slot].set(second_normed)

    def one_expert(operands):
        rows, gate_weight, up_weight = operands
        return gated_hidden(rows, gate_weight, up_weight)
    expert_hidden = lax.map(one_expert, (packed, expert_gate, expert_up))
    shared_hidden = gated_hidden(second_normed, shared_gate, shared_up)
    expert_block = HE // N_TENSOR
    shared_block = HS // N_TENSOR
    weights = route_gate.astype(jnp.float32)

    def final_add(summed, block_index):
        hidden_block = lax.dynamic_slice_in_dim(expert_hidden, block_index * expert_block, expert_block, 2).astype(jnp.float32)
        down_block = lax.dynamic_slice_in_dim(expert_down, block_index * expert_block, expert_block, 2).astype(jnp.float32)
        expert_out = jnp.einsum('ecf,edf->ecd', hidden_block, down_block)
        routed_block = rounded(expert_out)[expert_id, slot]
        shared_piece = lax.dynamic_slice_in_dim(shared_hidden, block_index * shared_block, shared_block, 1)
        shared_weight = lax.dynamic_slice_in_dim(shared_down, block_index * shared_block, shared_block, 1)
        shared_out = lax.dot_general(shared_piece, shared_weight, (((1,), (1,)), ((), ())), preferred_element_type=jnp.float32)
        return (summed + rounded(shared_out + weights * routed_block), None)
    summed, _ = lax.scan(final_add, jnp.zeros((TOKENS, D), jnp.float32), jnp.arange(N_TENSOR, dtype=jnp.int32))
    return (middle.astype(jnp.float32) + summed).astype(jnp.bfloat16)
```

```python
import jax
import jax.numpy as jnp
from jax import lax
from jax.experimental import pallas as pl
from jax.experimental.pallas import tpu as pltpu
from jax.sharding import PartitionSpec as P

EPSILON = 1e-05
MESH = pl.DeviceIdType.MESH
F32 = jnp.float32
BF16 = jnp.bfloat16

D = 2560
TOK = 128
FEAT = 160
ROWS = 80
HALF = D // 2
DEPTH = 8

NN = (((1,), (0,)), ((), ()))
NT = (((1,), (1,)), ((), ()))
TN = (((0,), (0,)), ((), ()))

PLANE = [(a, b) for a in range(4) for b in range(4) if (a, b) != (0, 0)]
PARTNERS = (
    [(a, b, 0, 0) for a, b in PLANE]
    + [(0, 0, d, 0) for d in (1, 2, 4, 8, 12, 14, 15)]
    + [(0, 0, 0, 1)]
)
NEAR = (1, 15, 2)
RING = (1, 3, 2)


def dot(a, b, dims):
    return lax.dot_general(a, b, dims, preferred_element_type=F32)


def identity(n):
    return (
        lax.broadcasted_iota(jnp.int32, (n, n), 0) == lax.broadcasted_iota(jnp.int32, (n, n), 1)
    ).astype(BF16)


def gated(gate_part, up_part):
    return (gate_part * jax.nn.sigmoid(gate_part) * up_part).astype(BF16)


N_SEM = 160


def kernel(
    tokens_ref, first_gain_ref, dense_gate_ref, dense_up_ref, dense_down_ref,
    second_gain_ref, shared_gate_ref, shared_up_ref, shared_down_ref,
    expert_gate_ref, expert_up_ref, expert_down_ref, routes_ref, route_gate_ref,
    out_ref,
    weights, staged, eg, eu, ed, ag0, ag1, xn, token_block, slot_matrix,
    routes_all, gates_all, part, sib0, sib1, sums0, sums1, near0, near1, mid0, mid1, far0, far1,
    accum, slots_out, slots_in, hidden_acc, expert_out, expert_sib, back_out, back_in, part1,
    send_sem, recv_sem, local_sem,
):
    e = lax.axis_index("expert")
    t = lax.axis_index("tensor")
    y, x, zh = e // 8, lax.rem(e // 2, 4), lax.rem(e, 2)
    z = zh * 8 + t // 2
    c = lax.rem(t, 2)
    zq, zr = z // 4, lax.rem(z, 4)
    other = 1 - zh
    oc = 1 - c

    def device(dy, dx, dz, dc):
        yy, xx = lax.rem(y + dy, 4), lax.rem(x + dx, 4)
        zz, cc = lax.rem(z + dz, 16), lax.rem(c + dc, 2)
        return {"expert": (yy * 4 + xx) * 2 + zz // 8, "tensor": lax.rem(zz, 8) * 2 + cc}

    counter = [0]
    pending = []

    def send(src, dst, offset):
        k = counter[0]
        counter[0] += 1
        copy = pltpu.make_async_remote_copy(
            src_ref=src,
            dst_ref=dst,
            send_sem=send_sem.at[k],
            recv_sem=recv_sem.at[k],
            device_id=device(*offset),
            device_id_type=MESH,
        )
        copy.start()
        pending.append(copy)
        return copy

    def landed(copies):
        for copy in copies:
            copy.wait_recv()

    loads = [
        pltpu.make_async_copy(src.at[0], dst, local_sem.at[i])
        for i, (src, dst) in enumerate(
            ((expert_gate_ref, eg), (expert_up_ref, eu), (expert_down_ref, ed))
        )
    ]
    for load in loads:
        load.start()

    barrier = pltpu.get_barrier_semaphore()
    for offset in PARTNERS:
        pl.semaphore_signal(barrier, inc=1, device_id=device(*offset), device_id_type=MESH)

    dense_refs = (dense_gate_ref, dense_up_ref, dense_down_ref)
    shared_refs = (shared_gate_ref, shared_up_ref, shared_down_ref)
    mine = pl.multiple_of(zh * 256, 256)
    theirs = pl.multiple_of(other * 256, 256)
    for i, ref in enumerate(dense_refs):
        for h in range(2):
            weights[3 * h + i, y, x, zh] = ref[:, pl.ds(mine + 128 * h, 128)]
            staged[3 * h + i] = ref[:, pl.ds(theirs + 128 * h, 128)]
    mine = pl.multiple_of(zh * 128, 128)
    theirs = pl.multiple_of(other * 128, 128)
    for i, ref in enumerate(shared_refs):
        weights[6 + i, y, x, zh] = ref[:, pl.ds(mine, 128)]
        staged[6 + i] = ref[:, pl.ds(theirs, 128)]
    tokens_t = dot(identity(FEAT), tokens_ref[...], NT).astype(BF16)
    token_block[...] = tokens_t
    ag0[zq, zr, c] = tokens_t

    routes_rows = jnp.broadcast_to(routes_ref[...].astype(F32), (TOK, TOK)).T
    gates_rows = jnp.broadcast_to(route_gate_ref[...], (TOK, TOK)).T
    routes_all[zh] = routes_rows[:8].astype(jnp.int32)
    gates_all[zh] = gates_rows[:8]

    pl.semaphore_wait(barrier, len(PARTNERS))

    def plane_first(unit, half, x_first):
        lo, n = unit
        block = weights.at[pl.ds(lo, n), y, x, half]
        return [
            send(block, block, (0, d, 0, 0) if x_first else (d, 0, 0, 0)) for d in RING
        ]

    def plane_second(unit, half, x_first):
        lo, n = unit
        if x_first:
            block = weights.at[pl.ds(lo, n), y, :, half]
            return [send(block, block, (d, 0, 0, 0)) for d in RING]
        block = weights.at[pl.ds(lo, n), :, x, half]
        return [send(block, block, (0, d, 0, 0)) for d in RING]

    A, B, S = (0, 3), (3, 3), (6, 3)

    def gather_far(buf):
        own = buf.at[zq, zr, c]
        return [send(own, own, (0, 0, d, 0)) for d in (8, 4, 12)]

    def gather_near(buf):
        block = buf.at[:, zr, c]
        return [send(block, block, (0, 0, d, 0)) for d in NEAR]

    def gather_sibling(buf):
        block = buf.at[:, :, c]
        return [send(block, block, (0, 0, 0, 1))]

    own_a = plane_first(A, zh, True)
    own_b = plane_first(B, zh, False)
    cross = [
        send(staged.at[pl.ds(lo, n)], weights.at[pl.ds(lo, n), y, x, zh], (0, 0, 8, 0))
        for lo, n in ((0, 6),)
    ]
    far = gather_far(ag0)
    cross_meta = [
        send(routes_all.at[zh], routes_all.at[zh], (0, 0, 8, 0)),
        send(gates_all.at[zh], gates_all.at[zh], (0, 0, 8, 0)),
    ]
    landed(own_a)
    own_a2 = plane_second(A, zh, True)
    landed(own_b)
    own_b2 = plane_second(B, zh, False)
    landed(cross)
    part_a = plane_first(A, other, True)
    part_b = plane_first(B, other, False)
    landed(far)
    near = gather_near(ag0)
    cross_s = [send(staged.at[pl.ds(6, 3)], weights.at[pl.ds(6, 3), y, x, zh], (0, 0, 8, 0))]
    landed(part_a)
    part_a2 = plane_second(A, other, True)
    landed(part_b)
    part_b2 = plane_second(B, other, False)
    own_s = plane_first(S, zh, True)

    landed(cross_meta)
    columns = []
    before = lax.broadcasted_iota(jnp.int32, (TOK, TOK), 0) < lax.broadcasted_iota(
        jnp.int32, (TOK, TOK), 1
    )
    for h in range(2):
        row = jnp.broadcast_to(routes_all[h][:1], (TOK, TOK))
        column = row.astype(F32).T.astype(jnp.int32)
        rank = jnp.sum(((row == column) & before).astype(F32), axis=0, keepdims=True)
        row = row[:1]
        slot = jnp.where((row & 1) == zh, (row >> 1) * 16 + h * DEPTH + rank.astype(jnp.int32), -1)
        columns.append(lax.broadcasted_iota(jnp.int32, (256, TOK), 0) == slot)
    slot_matrix[...] = jnp.concatenate(columns, axis=1).astype(F32).astype(BF16)

    def normalise(buf, gain_ref):
        eye = identity(TOK)
        squares = [jnp.zeros((TOK, 1), F32)] * 2
        for i in range(4):
            for h in range(2):
                block = buf[2 * h + i // 2, (2 * i) % 4 : (2 * i) % 4 + 2].reshape(640, TOK)
                rows = dot(eye, block, NT)
                xn[h * TOK : (h + 1) * TOK, 640 * i : 640 * (i + 1)] = rows.astype(BF16)
                squares[h] = squares[h] + jnp.sum(rows * rows, axis=1, keepdims=True)
        for h in range(2):
            scale = lax.rsqrt(squares[h] * (1.0 / D) + EPSILON)
            for i in range(4):
                at = (slice(h * TOK, (h + 1) * TOK), slice(640 * i, 640 * (i + 1)))
                gain = gain_ref[:, 640 * i : 640 * (i + 1)]
                xn[at] = (xn[at].astype(F32) * scale * gain).astype(BF16)

    landed(near)
    landed(gather_sibling(ag0))
    normalise(ag0, first_gain_ref)

    landed(own_a2 + own_b2 + part_a2 + part_b2)
    landed(cross_s)
    part_s = plane_first(S, other, False)

    def columns_of(blocks, yy):
        return jnp.concatenate([weights[b, yy].reshape(640, 128) for b in blocks], axis=1)

    hidden = jnp.zeros((256, 512), F32)
    for yy in range(4):
        hidden += dot(xn[:, 640 * yy : 640 * (yy + 1)], columns_of((0, 3, 1, 4), yy), NN)
    hidden = gated(hidden[:, :256], hidden[:, 256:])
    for zlo in range(8):
        rows = jnp.concatenate(
            [weights[b, zlo // 2, 2 * (zlo % 2) : 2 * (zlo % 2) + 2].reshape(320, 128) for b in (2, 5)],
            axis=1,
        )
        terms = dot(rows, hidden, NT).astype(BF16)
        for h in range(2):
            part[2 * h + zlo // 4, zlo % 4] = terms[:, h * TOK : (h + 1) * TOK].reshape(2, FEAT, TOK)

    landed(own_s)
    own_s2 = plane_second(S, zh, True)
    landed(part_s)
    part_s2 = plane_second(S, other, False)

    def reduce_scatter(part, sib, sums, near_in, mid, far_in):
        landed([send(part.at[:, :, oc], sib, (0, 0, 0, 1))])
        for q in range(4):
            for r in range(4):
                sums[q, r] = (part[q, r, c].astype(F32) + sib[q, r].astype(F32)).astype(BF16)
        landed(
            [
                send(sums.at[:, lax.rem(z + d, 4)], near_in.at[i], (0, 0, d, 0))
                for i, d in enumerate(NEAR)
            ]
        )
        for q in range(4):
            total = sums[q, zr].astype(F32)
            for i in range(3):
                total += near_in[i, q].astype(F32)
            mid[q] = total.astype(BF16)
        landed(
            [
                send(mid.at[lax.rem(zq + a, 4)], far_in.at[a - 1], (0, 0, 4 * a, 0))
                for a in (2, 1, 3)
            ]
        )
        total = mid[zq].astype(F32)
        for i in range(3):
            total += far_in[i].astype(F32)
        return total

    middle = token_block[...].astype(F32) + reduce_scatter(part, sib0, sums0, near0, mid0, far0)
    middle = middle.astype(BF16)
    token_block[...] = middle
    ag1[zq, zr, c] = middle
    landed(gather_far(ag1))
    landed(gather_near(ag1))
    landed(gather_sibling(ag1))
    normalise(ag1, second_gain_ref)

    half = pl.multiple_of(c * HALF, HALF)
    for i in range(5):
        piece = dot(slot_matrix[...], xn[:, pl.ds(half + 256 * i, 256)], NN)
        slots_out[:, 256 * i : 256 * (i + 1)] = piece.astype(BF16)

    def rows_of(yy, xx):
        return pl.ds(pl.multiple_of((yy * 4 + xx) * 16, 16), 16)

    own_rows = rows_of(y, x)

    def exchange(src, dst):
        return [
            send(
                src.at[rows_of(lax.rem(y + a, 4), lax.rem(x + b, 4))],
                dst.at[own_rows],
                (a, b, 0, 0),
            )
            for a, b in PLANE
        ]

    dispatched = exchange(slots_out, slots_in.at[c])
    slots_in[c, own_rows] = slots_out[own_rows]

    landed(own_s2 + part_s2)
    hidden = jnp.zeros((256, 256), F32)
    for yy in range(4):
        hidden += dot(xn[:, 640 * yy : 640 * (yy + 1)], columns_of((6, 7), yy), NN)
    hidden = gated(hidden[:, :128], hidden[:, 128:])
    for yy in range(4):
        accum[640 * yy : 640 * (yy + 1)] = dot(weights[8, yy].reshape(640, 128), hidden, NT)

    landed(dispatched)
    swapped = send(slots_in.at[c], slots_in.at[c], (0, 0, 0, 1))
    for load in loads:
        load.wait()

    def expert_half(h):
        base = pl.multiple_of(h * HALF, HALF)
        rows = slots_in.at[h]
        for i in range(5):
            k = pl.ds(base + 256 * i, 256)
            piece = rows[:, 256 * i : 256 * (i + 1)]
            hidden_acc[:, :256] += dot(piece, eg[k, :], NN)
            hidden_acc[:, 256:] += dot(piece, eu[k, :], NN)

    hidden_acc[...] = jnp.zeros_like(hidden_acc)
    expert_half(c)
    landed([swapped])
    expert_half(oc)
    hidden = gated(hidden_acc[:, :256], hidden_acc[:, 256:])
    for i in range(10):
        rows = dot(hidden, ed[256 * i : 256 * (i + 1), :], NT)
        expert_out[i // 5, :, 256 * (i % 5) : 256 * (i % 5 + 1)] = rows.astype(BF16)
    landed([send(expert_out.at[oc], expert_sib, (0, 0, 0, 1))])
    for i in range(5):
        at = (slice(None), slice(256 * i, 256 * (i + 1)))
        back_out[at] = (expert_out[c, :, 256 * i : 256 * (i + 1)].astype(F32) + expert_sib[at].astype(F32)).astype(BF16)
    returned = exchange(back_out, back_in)
    back_in[own_rows] = back_out[own_rows]
    landed(returned)

    gates = jnp.concatenate([gates_all[0][:1], gates_all[1][:1]], axis=1)
    for i in range(5):
        routed = dot(back_in[:, 256 * i : 256 * (i + 1)], slot_matrix[...], TN)
        accum[pl.ds(half + 256 * i, 256)] += routed * gates
    for zlo in range(8):
        terms = accum[320 * zlo : 320 * (zlo + 1)].astype(BF16)
        for h in range(2):
            part1[2 * h + zlo // 4, zlo % 4] = terms[:, h * TOK : (h + 1) * TOK].reshape(2, FEAT, TOK)
    mixed = token_block[...].astype(F32) + reduce_scatter(part1, sib1, sums1, near1, mid1, far1)
    out_ref[...] = dot(identity(TOK), mixed.astype(BF16), NT).astype(BF16)
    for copy in pending:
        copy.wait_send()


def local(*args):
    args = list(args)
    args[1] = args[1].reshape(1, D)
    args[5] = args[5].reshape(1, D)
    vmem = pl.BlockSpec(memory_space=pltpu.VMEM)
    anywhere = pl.BlockSpec(memory_space=pl.ANY)
    ring = (4, 4, FEAT, TOK)
    scratch = [
        ((9, 4, 4, 2, ROWS, 128), BF16),
        ((9, ROWS, 128), BF16),
        ((D, 256), BF16),
        ((D, 256), BF16),
        ((D, 256), BF16),
        ((4, 4, 2, FEAT, TOK), BF16),
        ((4, 4, 2, FEAT, TOK), BF16),
        ((256, D), BF16),
        ((FEAT, TOK), BF16),
        ((256, 256), BF16),
        ((2, 8, TOK), jnp.int32),
        ((2, 8, TOK), F32),
        ((4, 4, 2, FEAT, TOK), BF16),
        (ring, BF16),
        (ring, BF16),
        (ring, BF16),
        (ring, BF16),
        ((3, 4, FEAT, TOK), BF16),
        ((3, 4, FEAT, TOK), BF16),
        ((4, FEAT, TOK), BF16),
        ((4, FEAT, TOK), BF16),
        ((3, FEAT, TOK), BF16),
        ((3, FEAT, TOK), BF16),
        ((D, 256), F32),
        ((256, HALF), BF16),
        ((2, 256, HALF), BF16),
        ((256, 512), F32),
        ((2, 256, HALF), BF16),
        ((256, HALF), BF16),
        ((256, HALF), BF16),
        ((256, HALF), BF16),
        ((4, 4, 2, FEAT, TOK), BF16),
    ]
    return pl.pallas_call(
        kernel,
        out_shape=jax.ShapeDtypeStruct((TOK, FEAT), BF16),
        in_specs=[anywhere if 9 <= i < 12 else vmem for i in range(14)],
        out_specs=vmem,
        scratch_shapes=[pltpu.VMEM(shape, dtype) for shape, dtype in scratch]
        + [
            pltpu.SemaphoreType.DMA((N_SEM,)),
            pltpu.SemaphoreType.DMA((N_SEM,)),
            pltpu.SemaphoreType.DMA((3,)),
        ],
        compiler_params=pltpu.CompilerParams(
            collective_id=0, has_side_effects=True, vmem_limit_bytes=56 * 2**20
        ),
    )(*args)


def solution(mesh):
    placed = (
        P("expert", "tensor"),
        P(),
        P("expert", "tensor"),
        P("expert", "tensor"),
        P("expert", "tensor"),
        P(),
        P("expert", "tensor"),
        P("expert", "tensor"),
        P("expert", "tensor"),
        P("expert", None, "tensor"),
        P("expert", None, "tensor"),
        P("expert", None, "tensor"),
        P("expert", None),
        P("expert", None),
    )
    return jax.shard_map(
        local, mesh=mesh, in_specs=placed, out_specs=P("expert", "tensor"), check_vma=False
    )
```

```python
import jax
import jax.numpy as jnp
from jax import lax
from jax.experimental import pallas as pl
from jax.experimental.pallas import tpu as pltpu
from jax.sharding import PartitionSpec as P

EPSILON = 1e-05
MESH = pl.DeviceIdType.MESH
F32 = jnp.float32
BF16 = jnp.bfloat16

D = 2560
TOK = 128
FEAT = 160
ROWS = 80
HALF = D // 2
DEPTH = 8

NN = (((1,), (0,)), ((), ()))
NT = (((1,), (1,)), ((), ()))
TN = (((0,), (0,)), ((), ()))

PLANE = [(a, b) for a in range(4) for b in range(4) if (a, b) != (0, 0)]
PARTNERS = (
    [(a, b, 0, 0) for a, b in PLANE]
    + [(0, 0, d, 0) for d in (1, 2, 3, 8, 13, 14, 15)]
    + [(0, 0, 0, 1)]
)
RING = (1, 3, 2)


def dot(a, b, dims):
    return lax.dot_general(a, b, dims, preferred_element_type=F32)


def identity(n):
    return (
        lax.broadcasted_iota(jnp.int32, (n, n), 0) == lax.broadcasted_iota(jnp.int32, (n, n), 1)
    ).astype(BF16)


def gated(gate_part, up_part):
    return (gate_part * jax.nn.sigmoid(gate_part) * up_part).astype(BF16)


N_SEM = 256


def kernel(
    tokens_ref, first_gain_ref, dense_gate_ref, dense_up_ref, dense_down_ref,
    second_gain_ref, shared_gate_ref, shared_up_ref, shared_down_ref,
    expert_gate_ref, expert_up_ref, expert_down_ref, routes_ref, route_gate_ref,
    out_ref,
    weights, staged, eg, eu, ed, ag0, ag1, xn, token_block, slot_matrix,
    routes_all, gates_all, part, sib0, sib1, sums0, sums1, came0, came1, six, passed0, passed1,
    accum, slots_out, slots_in, hidden_acc, expert_out, expert_sib, back_out, back_in, part1,
    send_sem, recv_sem, local_sem,
):
    e = lax.axis_index("expert")
    t = lax.axis_index("tensor")
    y, x, zh = e // 8, lax.rem(e // 2, 4), lax.rem(e, 2)
    z = zh * 8 + t // 2
    c = lax.rem(t, 2)
    side = 1 - 2 * c
    other = 1 - zh
    oc = 1 - c

    def device(dy, dx, dz, dc):
        yy, xx = lax.rem(y + dy, 4), lax.rem(x + dx, 4)
        zz, cc = lax.rem(z + dz + 16, 16), lax.rem(c + dc, 2)
        return {"expert": (yy * 4 + xx) * 2 + zz // 8, "tensor": lax.rem(zz, 8) * 2 + cc}

    counter = [0]
    pending = []

    def send(src, dst, offset):
        k = counter[0]
        counter[0] += 1
        copy = pltpu.make_async_remote_copy(
            src_ref=src,
            dst_ref=dst,
            send_sem=send_sem.at[k],
            recv_sem=recv_sem.at[k],
            device_id=device(*offset),
            device_id_type=MESH,
        )
        copy.start()
        pending.append(copy)
        return copy

    def landed(copies):
        for copy in copies:
            copy.wait_recv()

    loads = [
        pltpu.make_async_copy(src.at[0], dst, local_sem.at[i])
        for i, (src, dst) in enumerate(
            ((expert_gate_ref, eg), (expert_up_ref, eu), (expert_down_ref, ed))
        )
    ]
    for load in loads:
        load.start()

    barrier = pltpu.get_barrier_semaphore()
    for offset in PARTNERS:
        pl.semaphore_signal(barrier, inc=1, device_id=device(*offset), device_id_type=MESH)

    dense_refs = (dense_gate_ref, dense_up_ref, dense_down_ref)
    shared_refs = (shared_gate_ref, shared_up_ref, shared_down_ref)
    mine = pl.multiple_of(zh * 256, 256)
    theirs = pl.multiple_of(other * 256, 256)
    for i, ref in enumerate(dense_refs):
        for h in range(2):
            weights[3 * h + i, y, x, zh] = ref[:, pl.ds(mine + 128 * h, 128)]
            staged[3 * h + i] = ref[:, pl.ds(theirs + 128 * h, 128)]
    mine = pl.multiple_of(zh * 128, 128)
    theirs = pl.multiple_of(other * 128, 128)
    for i, ref in enumerate(shared_refs):
        weights[6 + i, y, x, zh] = ref[:, pl.ds(mine, 128)]
        staged[6 + i] = ref[:, pl.ds(theirs, 128)]
    ag0[z, c] = tokens_ref[...]

    routes_all[zh] = jnp.broadcast_to(routes_ref[...], (8, TOK))
    gates_all[zh] = jnp.broadcast_to(route_gate_ref[...], (8, TOK))

    pl.semaphore_wait(barrier, len(PARTNERS))

    def plane_first(unit, half, x_first):
        lo, n = unit
        block = weights.at[pl.ds(lo, n), y, x, half]
        return [
            send(block, block, (0, d, 0, 0) if x_first else (d, 0, 0, 0)) for d in RING
        ]

    def plane_second(unit, half, x_first):
        lo, n = unit
        if x_first:
            block = weights.at[pl.ds(lo, n), y, :, half]
            return [send(block, block, (d, 0, 0, 0)) for d in RING]
        block = weights.at[pl.ds(lo, n), :, x, half]
        return [send(block, block, (0, d, 0, 0)) for d in RING]

    A, B, S = (0, 3), (3, 3), (6, 3)

    def spot(offset):
        return lax.rem(z + offset + 16, 16)

    def pass_on(buf, origin, steps):
        block = buf.at[spot(origin), c]
        return [send(block, block, (0, 0, step, 0)) for step in steps]

    def gather_start(buf):
        return pass_on(buf, 0, (3, -3, 1, -1)), pass_across(buf, (0,))

    def pass_across(buf, origins):
        blocks = [buf.at[spot(origin), c] for origin in origins]
        return [send(block, block, (0, 0, 0, 1)) for block in blocks]

    def gather_middle(buf, first, across):
        landed(first[:1])
        second = pass_on(buf, -3, (3, 1, -1))
        landed(first[1:2])
        second += pass_on(buf, 3, (-3, -1, 1))
        landed(first[2:])
        across += pass_across(buf, (-3, 3, -1, 1))
        return second

    def gather_end(buf, second, across):
        landed(second[:1])
        third = pass_on(buf, -6, (1, -1))
        landed(second[3:4])
        third += pass_on(buf, 6, (-1, 1))
        third += pass_on(buf, -6 * side, (2 * side,))
        landed(second[1:3] + second[4:])
        across += pass_across(buf, (-6, 6, -4, -2, 4, 2))
        landed(third)
        across += pass_across(buf, (-7, -5, 7, 5, 8))
        landed(across)

    own_a = plane_first(A, zh, True)
    own_b = plane_first(B, zh, False)
    def cross_over(lo, n):
        block = weights.at[pl.ds(lo, n), y, x, zh]
        return [send(staged.at[pl.ds(lo, n)], block, (0, 0, 8, 0))]

    order = (0, 1, 3, 4, 2, 5)
    cross = [cross_over(b, 1) for b in order]
    first, across = gather_start(ag0)
    cross_meta = [
        send(routes_all.at[zh], routes_all.at[zh], (0, 0, 8, 0)),
        send(gates_all.at[zh], gates_all.at[zh], (0, 0, 8, 0)),
    ]
    landed(own_a)
    own_a2 = plane_second(A, zh, True)
    landed(own_b)
    own_b2 = plane_second(B, zh, False)
    second = gather_middle(ag0, first, across)
    part_1, part_2 = {}, {}

    def crossed(i):
        landed(cross[i])
        part_1[i] = plane_first((order[i], 1), other, i % 2 == 0)

    def spread(i):
        landed(part_1[i])
        part_2[i] = plane_second((order[i], 1), other, i % 2 == 0)

    crossed(0)
    crossed(1)
    crossed(2)
    spread(0)
    crossed(3)
    spread(1)
    crossed(4)
    spread(2)
    crossed(5)
    spread(3)
    spread(4)
    spread(5)
    cross_s = cross_over(6, 3)
    own_s = plane_first(S, zh, True)
    gather_end(ag0, second, across)

    landed(cross_meta)
    columns = []
    before = lax.broadcasted_iota(jnp.int32, (TOK, TOK), 0) < lax.broadcasted_iota(
        jnp.int32, (TOK, TOK), 1
    )
    for h in range(2):
        row = jnp.broadcast_to(routes_all[h][:1], (TOK, TOK))
        column = row.astype(F32).T.astype(jnp.int32)
        rank = jnp.sum(((row == column) & before).astype(F32), axis=0, keepdims=True)
        row = row[:1]
        slot = jnp.where((row & 1) == zh, (row >> 1) * 16 + h * DEPTH + rank.astype(jnp.int32), -1)
        columns.append(lax.broadcasted_iota(jnp.int32, (256, TOK), 0) == slot)
    slot_matrix[...] = jnp.concatenate(columns, axis=1).astype(F32).astype(BF16)

    def normalise(buf, gain_ref):
        eye = identity(TOK)
        squares = [jnp.zeros((TOK, 1), F32)] * 2
        for i in range(4):
            for h in range(2):
                block = buf[8 * h + 2 * i : 8 * h + 2 * i + 2].reshape(640, TOK)
                rows = dot(eye, block, NT)
                xn[h * TOK : (h + 1) * TOK, 640 * i : 640 * (i + 1)] = rows.astype(BF16)
                squares[h] = squares[h] + jnp.sum(rows * rows, axis=1, keepdims=True)
        for h in range(2):
            scale = lax.rsqrt(squares[h] * (1.0 / D) + EPSILON)
            for i in range(4):
                at = (slice(h * TOK, (h + 1) * TOK), slice(640 * i, 640 * (i + 1)))
                gain = gain_ref[640 * i : 640 * (i + 1)][None, :]
                xn[at] = (xn[at].astype(F32) * scale * gain).astype(BF16)

    normalise(ag0, first_gain_ref)

    landed(own_a2 + own_b2)
    landed(part_2[0] + part_2[1] + part_2[2] + part_2[3])

    def columns_of(blocks, yy):
        return jnp.concatenate([weights[b, yy].reshape(640, 128) for b in blocks], axis=1)

    hidden = jnp.zeros((256, 512), F32)
    for yy in range(4):
        hidden += dot(xn[:, 640 * yy : 640 * (yy + 1)], columns_of((0, 3, 1, 4), yy), NN)
    hidden = gated(hidden[:, :256], hidden[:, 256:])
    landed(part_2[4] + part_2[5])
    for zlo in range(8):
        rows = jnp.concatenate(
            [weights[b, zlo // 2, 2 * (zlo % 2) : 2 * (zlo % 2) + 2].reshape(320, 128) for b in (2, 5)],
            axis=1,
        )
        terms = dot(rows, hidden, NT).astype(BF16)
        for h in range(2):
            part[8 * h + zlo] = terms[:, h * TOK : (h + 1) * TOK].reshape(2, FEAT, TOK)

    def reduce_scatter(part, sib, sums, came, six, passed, meanwhile):
        deep = (-7, -5, 7, 5, 8)
        middle = (-4, -2, 4, 2)
        rest = (-6, 6, -3, 3, -1, 1, 0)
        across = {
            o: send(part.at[spot(o), oc], sib.at[spot(o)], (0, 0, 0, 1)) for o in deep + middle + rest
        }

        def add_cores(o):
            landed([across[o]])
            i = spot(o)
            sums[i] = (part[i, c].astype(F32) + sib[i].astype(F32)).astype(BF16)

        slots = [0]

        def leave(o, step):
            slots[0] += 1
            slot = came.at[slots[0] - 1]
            return slots[0] - 1, send(sums.at[spot(o)], slot, (0, 0, step, 0))

        def arrived(*legs):
            landed([leg[1] for leg in legs])
            return sum(came[leg[0]].astype(F32) for leg in legs)

        legs = {}
        for o, step in zip(deep, (-1, 1, 1, -1, -2 * side)):
            add_cores(o)
            legs[o] = leave(o, step)
        for o, step in zip(middle, (-1, 1, 1, -1)):
            add_cores(o)
            legs[o] = leave(o, step)
        for o in rest:
            add_cores(o)
            if o in (-1, 1):
                legs[o] = leave(o, o)
        meanwhile()
        six[0] = sums[spot(-6)].astype(F32) + arrived(legs[-7], legs[-5])
        six[1] = sums[spot(6)].astype(F32) + arrived(legs[7], legs[5])
        six[c] += arrived(legs[8])
        for i, o in enumerate((-6, 6)):
            passed[i] = six[i].astype(BF16)
            slots[0] += 1
            slot = came.at[slots[0] - 1]
            legs[o] = (slots[0] - 1, send(passed.at[i], slot, (0, 0, -3 if o < 0 else 3, 0)))
        for i, s in enumerate((-1, 1)):
            three = sums[spot(3 * s)].astype(F32) + arrived(legs[2 * s], legs[4 * s]) + arrived(legs[6 * s])
            passed[2 + i] = three.astype(BF16)
            slots[0] += 1
            slot = came.at[slots[0] - 1]
            legs[3 * s] = (slots[0] - 1, send(passed.at[2 + i], slot, (0, 0, 3 * s, 0)))
        total = sums[z].astype(F32) + arrived(legs[-1], legs[1])
        return total + arrived(legs[-3], legs[3])

    late = {}

    def shared_weights():
        landed(cross_s)
        late["part"] = plane_first(S, other, False)
        landed(own_s)
        late["own"] = plane_second(S, zh, True)

    middle = reduce_scatter(part, sib0, sums0, came0, six, passed0, shared_weights)
    middle = (tokens_ref[...].astype(F32) + middle).astype(BF16)
    token_block[...] = middle
    ag1[z, c] = middle
    first, across = gather_start(ag1)
    landed(late["part"])
    part_s2 = plane_second(S, other, False)
    second = gather_middle(ag1, first, across)
    gather_end(ag1, second, across)
    normalise(ag1, second_gain_ref)

    half = pl.multiple_of(c * HALF, HALF)
    for i in range(5):
        piece = dot(slot_matrix[...], xn[:, pl.ds(half + 256 * i, 256)], NN)
        slots_out[:, 256 * i : 256 * (i + 1)] = piece.astype(BF16)

    def rows_of(yy, xx):
        return pl.ds(pl.multiple_of((yy * 4 + xx) * 16, 16), 16)

    own_rows = rows_of(y, x)

    def exchange(src, dst):
        return [
            send(
                src.at[rows_of(lax.rem(y + a, 4), lax.rem(x + b, 4))],
                dst.at[own_rows],
                (a, b, 0, 0),
            )
            for a, b in PLANE
        ]

    dispatched = exchange(slots_out, slots_in.at[c])
    slots_in[c, own_rows] = slots_out[own_rows]

    landed(late["own"] + part_s2)
    hidden = jnp.zeros((256, 256), F32)
    for yy in range(4):
        hidden += dot(xn[:, 640 * yy : 640 * (yy + 1)], columns_of((6, 7), yy), NN)
    hidden = gated(hidden[:, :128], hidden[:, 128:])
    for yy in range(4):
        accum[640 * yy : 640 * (yy + 1)] = dot(weights[8, yy].reshape(640, 128), hidden, NT)

    landed(dispatched)
    swapped = send(slots_in.at[c], slots_in.at[c], (0, 0, 0, 1))
    for load in loads:
        load.wait()

    def expert_half(h):
        base = pl.multiple_of(h * HALF, HALF)
        rows = slots_in.at[h]
        for i in range(5):
            k = pl.ds(base + 256 * i, 256)
            piece = rows[:, 256 * i : 256 * (i + 1)]
            hidden_acc[:, :256] += dot(piece, eg[k, :], NN)
            hidden_acc[:, 256:] += dot(piece, eu[k, :], NN)

    hidden_acc[...] = jnp.zeros_like(hidden_acc)
    expert_half(c)
    landed([swapped])
    expert_half(oc)
    hidden = gated(hidden_acc[:, :256], hidden_acc[:, 256:])
    for i in range(10):
        rows = dot(hidden, ed[256 * i : 256 * (i + 1), :], NT)
        expert_out[i // 5, :, 256 * (i % 5) : 256 * (i % 5 + 1)] = rows.astype(BF16)
    landed([send(expert_out.at[oc], expert_sib, (0, 0, 0, 1))])
    for i in range(5):
        at = (slice(None), slice(256 * i, 256 * (i + 1)))
        back_out[at] = (expert_out[c, :, 256 * i : 256 * (i + 1)].astype(F32) + expert_sib[at].astype(F32)).astype(BF16)
    returned = exchange(back_out, back_in)
    back_in[own_rows] = back_out[own_rows]
    landed(returned)

    gates = jnp.concatenate([gates_all[0][:1], gates_all[1][:1]], axis=1)
    for i in range(5):
        routed = dot(back_in[:, 256 * i : 256 * (i + 1)], slot_matrix[...], TN)
        accum[pl.ds(half + 256 * i, 256)] += routed * gates
    for zlo in range(8):
        terms = accum[320 * zlo : 320 * (zlo + 1)].astype(BF16)
        for h in range(2):
            part1[8 * h + zlo] = terms[:, h * TOK : (h + 1) * TOK].reshape(2, FEAT, TOK)
    mixed = reduce_scatter(part1, sib1, sums1, came1, six, passed1, lambda: None)
    mixed = token_block[...].astype(F32) + mixed
    out_ref[...] = mixed.astype(BF16)
    for copy in pending:
        copy.wait_send()


def local(*args):
    args = list(args)
    args[0] = args[0].T
    args[12] = args[12].reshape(1, TOK)
    args[13] = args[13].reshape(1, TOK)
    vmem = pl.BlockSpec(memory_space=pltpu.VMEM)
    anywhere = pl.BlockSpec(memory_space=pl.ANY)
    ring = (16, FEAT, TOK)
    scratch = [
        ((9, 4, 4, 2, ROWS, 128), BF16),
        ((9, ROWS, 128), BF16),
        ((D, 256), BF16),
        ((D, 256), BF16),
        ((D, 256), BF16),
        ((16, 2, FEAT, TOK), BF16),
        ((16, 2, FEAT, TOK), BF16),
        ((256, D), BF16),
        ((FEAT, TOK), BF16),
        ((256, 256), BF16),
        ((2, 8, TOK), jnp.int32),
        ((2, 8, TOK), F32),
        ((16, 2, FEAT, TOK), BF16),
        (ring, BF16),
        (ring, BF16),
        (ring, BF16),
        (ring, BF16),
        ((15, FEAT, TOK), BF16),
        ((15, FEAT, TOK), BF16),
        ((2, FEAT, TOK), F32),
        ((4, FEAT, TOK), BF16),
        ((4, FEAT, TOK), BF16),
        ((D, 256), F32),
        ((256, HALF), BF16),
        ((2, 256, HALF), BF16),
        ((256, 512), F32),
        ((2, 256, HALF), BF16),
        ((256, HALF), BF16),
        ((256, HALF), BF16),
        ((256, HALF), BF16),
        ((16, 2, FEAT, TOK), BF16),
    ]
    return pl.pallas_call(
        kernel,
        out_shape=jax.ShapeDtypeStruct((FEAT, TOK), BF16),
        in_specs=[anywhere if 9 <= i < 12 else vmem for i in range(14)],
        out_specs=vmem,
        scratch_shapes=[pltpu.VMEM(shape, dtype) for shape, dtype in scratch]
        + [
            pltpu.SemaphoreType.DMA((N_SEM,)),
            pltpu.SemaphoreType.DMA((N_SEM,)),
            pltpu.SemaphoreType.DMA((3,)),
        ],
        compiler_params=pltpu.CompilerParams(
            collective_id=0, has_side_effects=True, vmem_limit_bytes=56 * 2**20
        ),
    )(*args).T


def solution(mesh):
    placed = (
        P("expert", "tensor"),
        P(),
        P("expert", "tensor"),
        P("expert", "tensor"),
        P("expert", "tensor"),
        P(),
        P("expert", "tensor"),
        P("expert", "tensor"),
        P("expert", "tensor"),
        P("expert", None, "tensor"),
        P("expert", None, "tensor"),
        P("expert", None, "tensor"),
        P("expert", None),
        P("expert", None),
    )
    return jax.shard_map(
        local, mesh=mesh, in_specs=placed, out_specs=P("expert", "tensor"), check_vma=False
    )
```

```python
import jax
import jax.numpy as jnp
from jax import lax
from jax.experimental import pallas as pl
from jax.experimental.pallas import tpu as pltpu
from jax.sharding import PartitionSpec as P

EPSILON = 1e-05
MESH = pl.DeviceIdType.MESH
F32 = jnp.float32
BF16 = jnp.bfloat16

D = 2560
TOK = 128
FEAT = 160
ROWS = 80
HALF = D // 2
DEPTH = 8

NN = (((1,), (0,)), ((), ()))
NT = (((1,), (1,)), ((), ()))
TN = (((0,), (0,)), ((), ()))

PLANE = sorted(
    [(a, b) for a in range(4) for b in range(4) if (a, b) != (0, 0)],
    key=lambda place: -min(place[0], 4 - place[0]) - min(place[1], 4 - place[1]),
)
PARTNERS = (
    [(a, b, 0, 0) for a, b in PLANE]
    + [(0, 0, d, 0) for d in (1, 2, 3, 8, 13, 14, 15)]
    + [(0, 0, 0, 1)]
)
RING = (1, 3, 2)


def dot(a, b, dims):
    return lax.dot_general(a, b, dims, preferred_element_type=F32)


def identity(n):
    return (
        lax.broadcasted_iota(jnp.int32, (n, n), 0) == lax.broadcasted_iota(jnp.int32, (n, n), 1)
    ).astype(BF16)


def gated(gate_part, up_part):
    return (gate_part * jax.nn.sigmoid(gate_part) * up_part).astype(BF16)


N_SEM = 320


def kernel(
    tokens_ref, first_gain_ref, dense_gate_ref, dense_up_ref, dense_down_ref,
    second_gain_ref, shared_gate_ref, shared_up_ref, shared_down_ref,
    expert_gate_ref, expert_up_ref, expert_down_ref, routes_ref, route_gate_ref,
    out_ref,
    weights, staged, eg, eu, ed, ag0, ag1, xn, token_block, slot_matrix,
    routes_all, gates_all, part, sib0, sib1, sums0, sums1, came0, came1, six, passed0, passed1,
    accum, slots_out, slots_in, hidden_acc, expert_out, expert_sib, back_out, back_in, part1,
    send_sem, recv_sem, local_sem,
):
    e = lax.axis_index("expert")
    t = lax.axis_index("tensor")
    y, x, zh = e // 8, lax.rem(e // 2, 4), lax.rem(e, 2)
    z = zh * 8 + t // 2
    c = lax.rem(t, 2)
    side = 1 - 2 * c
    other = 1 - zh
    oc = 1 - c

    def device(dy, dx, dz, dc):
        yy, xx = lax.rem(y + dy, 4), lax.rem(x + dx, 4)
        zz, cc = lax.rem(z + dz + 16, 16), lax.rem(c + dc, 2)
        return {"expert": (yy * 4 + xx) * 2 + zz // 8, "tensor": lax.rem(zz, 8) * 2 + cc}

    counter = [0]
    pending = []

    def send(src, dst, offset):
        k = counter[0]
        counter[0] += 1
        copy = pltpu.make_async_remote_copy(
            src_ref=src,
            dst_ref=dst,
            send_sem=send_sem.at[k],
            recv_sem=recv_sem.at[k],
            device_id=device(*offset),
            device_id_type=MESH,
        )
        copy.start()
        pending.append(copy)
        return copy

    def landed(copies):
        for copy in copies:
            copy.wait_recv()

    loads = [
        pltpu.make_async_copy(src.at[0], dst, local_sem.at[i])
        for i, (src, dst) in enumerate(
            ((expert_gate_ref, eg), (expert_up_ref, eu), (expert_down_ref, ed))
        )
    ]
    for load in loads:
        load.start()

    barrier = pltpu.get_barrier_semaphore()
    for offset in PARTNERS:
        pl.semaphore_signal(barrier, inc=1, device_id=device(*offset), device_id_type=MESH)

    dense_refs = (dense_gate_ref, dense_up_ref, dense_down_ref)
    shared_refs = (shared_gate_ref, shared_up_ref, shared_down_ref)
    mine = pl.multiple_of(zh * 256, 256)
    theirs = pl.multiple_of(other * 256, 256)
    for i, ref in enumerate(dense_refs):
        for h in range(2):
            weights[3 * h + i, y, x, zh] = ref[:, pl.ds(mine + 128 * h, 128)]
            staged[3 * h + i] = ref[:, pl.ds(theirs + 128 * h, 128)]
    mine = pl.multiple_of(zh * 128, 128)
    theirs = pl.multiple_of(other * 128, 128)
    for i, ref in enumerate(shared_refs):
        weights[6 + i, y, x, zh] = ref[:, pl.ds(mine, 128)]
        staged[6 + i] = ref[:, pl.ds(theirs, 128)]
    ag0[z, c] = tokens_ref[...]

    routes_all[zh] = jnp.broadcast_to(routes_ref[...], (8, TOK))
    gates_all[zh] = jnp.broadcast_to(route_gate_ref[...], (8, TOK))

    pl.semaphore_wait(barrier, len(PARTNERS))

    def plane_first(unit, half, x_first):
        lo, n = unit
        block = weights.at[pl.ds(lo, n), y, x, half]
        return [
            send(block, block, (0, d, 0, 0) if x_first else (d, 0, 0, 0)) for d in RING
        ]

    def plane_second(unit, half, x_first):
        lo, n = unit
        if x_first:
            block = weights.at[pl.ds(lo, n), y, :, half]
            return [send(block, block, (d, 0, 0, 0)) for d in RING]
        block = weights.at[pl.ds(lo, n), :, x, half]
        return [send(block, block, (0, d, 0, 0)) for d in RING]

    A, B, S = (0, 3), (3, 3), (6, 3)

    def spot(offset):
        return lax.rem(z + offset + 16, 16)

    def pass_on(buf, origin, steps):
        block = buf.at[spot(origin), c]
        return [send(block, block, (0, 0, step, 0)) for step in steps]

    def gather_start(buf):
        return pass_on(buf, 0, (3, -3, 1, -1)), pass_across(buf, (0,))

    def pass_across(buf, origins):
        blocks = [buf.at[spot(origin), c] for origin in origins]
        return [send(block, block, (0, 0, 0, 1)) for block in blocks]

    def gather_middle(buf, first, across):
        landed(first[:1])
        second = pass_on(buf, -3, (3, 1, -1))
        landed(first[1:2])
        second += pass_on(buf, 3, (-3, -1, 1))
        landed(first[2:])
        across += pass_across(buf, (-3, 3, -1, 1))
        return second

    def gather_late(buf, second, across):
        landed(second[:1])
        third = pass_on(buf, -6, (1, -1))
        landed(second[3:4])
        third += pass_on(buf, 6, (-1, 1))
        third += pass_on(buf, -6 * side, (2 * side,))
        landed(second[1:3] + second[4:])
        across += pass_across(buf, (-6, 6, -4, -2, 4, 2))
        return third

    def gather_end(buf, third, across):
        landed(third)
        across += pass_across(buf, (-7, -5, 7, 5, 8))
        landed(across)

    def plane_beside(unit, half, x_first):
        lo, n = unit
        if x_first:
            block = weights.at[pl.ds(lo, n), y, :, half]
            return [send(block, block, (d, 0, 0, 0)) for d in (1, 3)]
        block = weights.at[pl.ds(lo, n), :, x, half]
        return [send(block, block, (0, d, 0, 0)) for d in (1, 3)]

    def plane_beyond(unit, half, x_first, beside):
        lo, n = unit
        passed_on = []
        for copy, d, rows in zip(beside, (1, 3), (slice(0, 2), slice(2, 4))):
            landed([copy])
            if x_first:
                block = weights.at[pl.ds(lo, n), lax.rem(y + 4 - d, 4), rows, half]
                passed_on.append(send(block, block, (d, 0, 0, 0)))
            else:
                block = weights.at[pl.ds(lo, n), rows, lax.rem(x + 4 - d, 4), half]
                passed_on.append(send(block, block, (0, d, 0, 0)))
        return passed_on

    def cross_over(lo, n):
        block = weights.at[pl.ds(lo, n), y, x, zh]
        return [send(staged.at[pl.ds(lo, n)], block, (0, 0, 8, 0))]

    first, across = gather_start(ag0)
    own_a = plane_first(A, zh, True)
    own_b = plane_first(B, zh, False)
    order = (0, 1, 3, 4, 2, 5)
    cross = [cross_over(b, 1) for b in order]
    cross_meta = [
        send(routes_all.at[zh], routes_all.at[zh], (0, 0, 8, 0)),
        send(gates_all.at[zh], gates_all.at[zh], (0, 0, 8, 0)),
    ]
    part_1, part_2, part_3 = {}, {}, {}

    def crossed(i):
        landed(cross[i])
        part_1[i] = plane_first((order[i], 1), other, i % 2 == 0)

    def beside(i):
        landed(part_1[i])
        part_2[i] = plane_beside((order[i], 1), other, i % 2 == 0)

    def beyond(i):
        part_3[i] = plane_beyond((order[i], 1), other, i % 2 == 0, part_2[i])

    landed(own_a)
    own_a2 = plane_beside(A, zh, True)
    landed(own_b)
    own_b2 = plane_beside(B, zh, False)
    second = gather_middle(ag0, first, across)
    crossed(0)
    crossed(1)
    crossed(2)
    beside(0)
    crossed(3)
    beside(1)
    crossed(4)
    own_3 = plane_beyond(A, zh, True, own_a2) + plane_beyond(B, zh, False, own_b2)
    third = gather_late(ag0, second, across)
    cross_s = cross_over(6, 3)
    beside(2)
    crossed(5)
    beside(3)
    beyond(0)
    beside(4)
    beyond(1)
    beside(5)
    for i in range(2, 6):
        beyond(i)
    own_s = plane_first(S, zh, True)
    gather_end(ag0, third, across)

    landed(cross_meta)
    columns = []
    before = lax.broadcasted_iota(jnp.int32, (TOK, TOK), 0) < lax.broadcasted_iota(
        jnp.int32, (TOK, TOK), 1
    )
    for h in range(2):
        row = jnp.broadcast_to(routes_all[h][:1], (TOK, TOK))
        column = row.astype(F32).T.astype(jnp.int32)
        rank = jnp.sum(((row == column) & before).astype(F32), axis=0, keepdims=True)
        row = row[:1]
        slot = jnp.where((row & 1) == zh, (row >> 1) * 16 + h * DEPTH + rank.astype(jnp.int32), -1)
        columns.append(lax.broadcasted_iota(jnp.int32, (256, TOK), 0) == slot)
    slot_matrix[...] = jnp.concatenate(columns, axis=1).astype(F32).astype(BF16)

    def normalise(buf, gain_ref):
        eye = identity(TOK)
        squares = [jnp.zeros((TOK, 1), F32)] * 2
        for i in range(4):
            for h in range(2):
                block = buf[8 * h + 2 * i : 8 * h + 2 * i + 2].reshape(640, TOK)
                rows = dot(eye, block, NT)
                xn[h * TOK : (h + 1) * TOK, 640 * i : 640 * (i + 1)] = rows.astype(BF16)
                squares[h] = squares[h] + jnp.sum(rows * rows, axis=1, keepdims=True)
        for h in range(2):
            scale = lax.rsqrt(squares[h] * (1.0 / D) + EPSILON)
            for i in range(4):
                at = (slice(h * TOK, (h + 1) * TOK), slice(640 * i, 640 * (i + 1)))
                gain = gain_ref[640 * i : 640 * (i + 1)][None, :]
                xn[at] = (xn[at].astype(F32) * scale * gain).astype(BF16)

    normalise(ag0, first_gain_ref)

    landed(own_3 + part_3[0] + part_3[1] + part_3[2] + part_3[3])

    def columns_of(blocks, yy):
        return jnp.concatenate([weights[b, yy].reshape(640, 128) for b in blocks], axis=1)

    hidden = jnp.zeros((256, 512), F32)
    for yy in range(4):
        hidden += dot(xn[:, 640 * yy : 640 * (yy + 1)], columns_of((0, 3, 1, 4), yy), NN)
    hidden = gated(hidden[:, :256], hidden[:, 256:])
    landed(part_3[4] + part_3[5])
    for zlo in range(8):
        rows = jnp.concatenate(
            [weights[b, zlo // 2, 2 * (zlo % 2) : 2 * (zlo % 2) + 2].reshape(320, 128) for b in (2, 5)],
            axis=1,
        )
        terms = dot(rows, hidden, NT).astype(BF16)
        for h in range(2):
            part[8 * h + zlo] = terms[:, h * TOK : (h + 1) * TOK].reshape(2, FEAT, TOK)

    def reduce_scatter(part, sib, sums, came, six, passed, meanwhile):
        deep = (-7, -5, 7, 5, 8)
        middle = (-4, -2, 4, 2)
        rest = (-6, 6, -3, 3, -1, 1, 0)
        across = {
            o: send(part.at[spot(o), oc], sib.at[spot(o)], (0, 0, 0, 1)) for o in deep + middle + rest
        }

        def add_cores(o):
            landed([across[o]])
            i = spot(o)
            sums[i] = (part[i, c].astype(F32) + sib[i].astype(F32)).astype(BF16)

        slots = [0]

        def leave(o, step):
            slots[0] += 1
            slot = came.at[slots[0] - 1]
            return slots[0] - 1, send(sums.at[spot(o)], slot, (0, 0, step, 0))

        def arrived(*legs):
            landed([leg[1] for leg in legs])
            return sum(came[leg[0]].astype(F32) for leg in legs)

        legs = {}
        for o, step in zip(deep, (-1, 1, 1, -1, -2 * side)):
            add_cores(o)
            legs[o] = leave(o, step)
        for o, step in zip(middle, (-1, 1, 1, -1)):
            add_cores(o)
            legs[o] = leave(o, step)
        for o in rest:
            add_cores(o)
            if o in (-1, 1):
                legs[o] = leave(o, o)
        six[0] = sums[spot(-6)].astype(F32) + arrived(legs[-7], legs[-5])
        six[1] = sums[spot(6)].astype(F32) + arrived(legs[7], legs[5])
        six[c] += arrived(legs[8])
        for i, o in enumerate((-6, 6)):
            passed[i] = six[i].astype(BF16)
            slots[0] += 1
            slot = came.at[slots[0] - 1]
            legs[o] = (slots[0] - 1, send(passed.at[i], slot, (0, 0, -3 if o < 0 else 3, 0)))
        meanwhile()
        for i, s in enumerate((-1, 1)):
            three = sums[spot(3 * s)].astype(F32) + arrived(legs[2 * s], legs[4 * s]) + arrived(legs[6 * s])
            passed[2 + i] = three.astype(BF16)
            slots[0] += 1
            slot = came.at[slots[0] - 1]
            legs[3 * s] = (slots[0] - 1, send(passed.at[2 + i], slot, (0, 0, 3 * s, 0)))
        total = sums[z].astype(F32) + arrived(legs[-1], legs[1])
        return total + arrived(legs[-3], legs[3])

    late = {}

    def shared_weights():
        landed(cross_s)
        late["part"] = plane_first(S, other, False)
        landed(own_s)
        late["own"] = plane_second(S, zh, True)

    middle = reduce_scatter(part, sib0, sums0, came0, six, passed0, shared_weights)
    middle = (tokens_ref[...].astype(F32) + middle).astype(BF16)
    token_block[...] = middle
    ag1[z, c] = middle
    first, across = gather_start(ag1)
    landed(late["part"])
    part_s2 = plane_second(S, other, False)
    second = gather_middle(ag1, first, across)
    third = gather_late(ag1, second, across)
    gather_end(ag1, third, across)
    normalise(ag1, second_gain_ref)

    half = pl.multiple_of(c * HALF, HALF)
    for i in range(5):
        piece = dot(slot_matrix[...], xn[:, pl.ds(half + 256 * i, 256)], NN)
        slots_out[:, 256 * i : 256 * (i + 1)] = piece.astype(BF16)

    def rows_of(yy, xx):
        return pl.ds(pl.multiple_of((yy * 4 + xx) * 16, 16), 16)

    own_rows = rows_of(y, x)

    def exchange(src, dst):
        return [
            send(
                src.at[rows_of(lax.rem(y + a, 4), lax.rem(x + b, 4))],
                dst.at[own_rows],
                (a, b, 0, 0),
            )
            for a, b in PLANE
        ]

    dispatched = exchange(slots_out, slots_in.at[c])
    slots_in[c, own_rows] = slots_out[own_rows]

    landed(late["own"] + part_s2)
    hidden = jnp.zeros((256, 256), F32)
    for yy in range(4):
        hidden += dot(xn[:, 640 * yy : 640 * (yy + 1)], columns_of((6, 7), yy), NN)
    hidden = gated(hidden[:, :128], hidden[:, 128:])
    for yy in range(4):
        accum[640 * yy : 640 * (yy + 1)] = dot(weights[8, yy].reshape(640, 128), hidden, NT)

    swapped = []
    for k, (a, b) in enumerate([(0, 0)] + PLANE):
        if k:
            landed(dispatched[k - 1 : k])
        block = slots_in.at[c, rows_of(lax.rem(y + 4 - a, 4), lax.rem(x + 4 - b, 4))]
        swapped.append(send(block, block, (0, 0, 0, 1)))
    for load in loads:
        load.wait()

    def expert_half(h):
        base = pl.multiple_of(h * HALF, HALF)
        rows = slots_in.at[h]
        for i in range(5):
            k = pl.ds(base + 256 * i, 256)
            piece = rows[:, 256 * i : 256 * (i + 1)]
            hidden_acc[:, :256] += dot(piece, eg[k, :], NN)
            hidden_acc[:, 256:] += dot(piece, eu[k, :], NN)

    hidden_acc[...] = jnp.zeros_like(hidden_acc)
    expert_half(c)
    landed(swapped)
    expert_half(oc)
    hidden = gated(hidden_acc[:, :256], hidden_acc[:, 256:])
    def expert_rows(h, i):
        k = pl.ds(pl.multiple_of(h * HALF, HALF) + 256 * i, 256)
        return dot(hidden, ed[k, :], NT)

    crossing = []
    for i in range(5):
        cols = slice(256 * i, 256 * (i + 1))
        expert_out[:, cols] = expert_rows(oc, i).astype(BF16)
        crossing.append(send(expert_out.at[:, cols], expert_sib.at[:, cols], (0, 0, 0, 1)))
    for i in range(5):
        cols = slice(256 * i, 256 * (i + 1))
        rows = expert_rows(c, i)
        landed(crossing[i : i + 1])
        back_out[:, cols] = (rows + expert_sib[:, cols].astype(F32)).astype(BF16)
    returned = exchange(back_out, back_in)
    back_in[own_rows] = back_out[own_rows]
    landed(returned)

    gates = jnp.concatenate([gates_all[0][:1], gates_all[1][:1]], axis=1)
    for i in range(5):
        routed = dot(back_in[:, 256 * i : 256 * (i + 1)], slot_matrix[...], TN)
        accum[pl.ds(half + 256 * i, 256)] += routed * gates
    for zlo in range(8):
        terms = accum[320 * zlo : 320 * (zlo + 1)].astype(BF16)
        for h in range(2):
            part1[8 * h + zlo] = terms[:, h * TOK : (h + 1) * TOK].reshape(2, FEAT, TOK)
    mixed = reduce_scatter(part1, sib1, sums1, came1, six, passed1, lambda: None)
    mixed = token_block[...].astype(F32) + mixed
    out_ref[...] = mixed.astype(BF16)
    assert counter[0] <= N_SEM
    for copy in pending:
        copy.wait_send()


def local(*args):
    args = list(args)
    args[0] = args[0].T
    args[12] = args[12].reshape(1, TOK)
    args[13] = args[13].reshape(1, TOK)
    vmem = pl.BlockSpec(memory_space=pltpu.VMEM)
    anywhere = pl.BlockSpec(memory_space=pl.ANY)
    ring = (16, FEAT, TOK)
    scratch = [
        ((9, 4, 4, 2, ROWS, 128), BF16),
        ((9, ROWS, 128), BF16),
        ((D, 256), BF16),
        ((D, 256), BF16),
        ((D, 256), BF16),
        ((16, 2, FEAT, TOK), BF16),
        ((16, 2, FEAT, TOK), BF16),
        ((256, D), BF16),
        ((FEAT, TOK), BF16),
        ((256, 256), BF16),
        ((2, 8, TOK), jnp.int32),
        ((2, 8, TOK), F32),
        ((16, 2, FEAT, TOK), BF16),
        (ring, BF16),
        (ring, BF16),
        (ring, BF16),
        (ring, BF16),
        ((15, FEAT, TOK), BF16),
        ((15, FEAT, TOK), BF16),
        ((2, FEAT, TOK), F32),
        ((4, FEAT, TOK), BF16),
        ((4, FEAT, TOK), BF16),
        ((D, 256), F32),
        ((256, HALF), BF16),
        ((2, 256, HALF), BF16),
        ((256, 512), F32),
        ((256, HALF), BF16),
        ((256, HALF), BF16),
        ((256, HALF), BF16),
        ((256, HALF), BF16),
        ((16, 2, FEAT, TOK), BF16),
    ]
    return pl.pallas_call(
        kernel,
        out_shape=jax.ShapeDtypeStruct((FEAT, TOK), BF16),
        in_specs=[anywhere if 9 <= i < 12 else vmem for i in range(14)],
        out_specs=vmem,
        scratch_shapes=[pltpu.VMEM(shape, dtype) for shape, dtype in scratch]
        + [
            pltpu.SemaphoreType.DMA((N_SEM,)),
            pltpu.SemaphoreType.DMA((N_SEM,)),
            pltpu.SemaphoreType.DMA((3,)),
        ],
        compiler_params=pltpu.CompilerParams(
            collective_id=0, has_side_effects=True, vmem_limit_bytes=56 * 2**20
        ),
    )(*args).T


def solution(mesh):
    placed = (
        P("expert", "tensor"),
        P(),
        P("expert", "tensor"),
        P("expert", "tensor"),
        P("expert", "tensor"),
        P(),
        P("expert", "tensor"),
        P("expert", "tensor"),
        P("expert", "tensor"),
        P("expert", None, "tensor"),
        P("expert", None, "tensor"),
        P("expert", None, "tensor"),
        P("expert", None),
        P("expert", None),
    )
    return jax.shard_map(
        local, mesh=mesh, in_specs=placed, out_specs=P("expert", "tensor"), check_vma=False
    )
```

```python
import jax
import jax.numpy as jnp
from jax import lax
from jax.experimental import pallas as pl
from jax.experimental.pallas import tpu as pltpu
from jax.sharding import PartitionSpec as P

EPSILON = 1e-05
MESH = pl.DeviceIdType.MESH
F32 = jnp.float32
BF16 = jnp.bfloat16

D = 2560
TOK = 128
FEAT = 160
ROWS = 80
HALF = D // 2
DEPTH = 8

NN = (((1,), (0,)), ((), ()))
NT = (((1,), (1,)), ((), ()))
TN = (((0,), (0,)), ((), ()))

PLANE = sorted(
    [(a, b) for a in range(4) for b in range(4) if (a, b) != (0, 0)],
    key=lambda place: -min(place[0], 4 - place[0]) - min(place[1], 4 - place[1]),
)
PARTNERS = (
    [(a, b, 0, 0) for a, b in PLANE]
    + [(0, 0, d, 0) for d in (1, 2, 3, 8, 13, 14, 15)]
    + [(0, 0, 0, 1)]
)
RING = (1, 3, 2)
HALVES = (slice(0, 80), slice(80, 160))


def dot(a, b, dims):
    return lax.dot_general(a, b, dims, preferred_element_type=F32)


def identity(n):
    return (
        lax.broadcasted_iota(jnp.int32, (n, n), 0) == lax.broadcasted_iota(jnp.int32, (n, n), 1)
    ).astype(BF16)


def gated(gate_part, up_part):
    return (gate_part * jax.nn.sigmoid(gate_part) * up_part).astype(BF16)


N_SEM = 320


def kernel(
    tokens_ref, first_gain_ref, dense_gate_ref, dense_up_ref, dense_down_ref,
    second_gain_ref, shared_gate_ref, shared_up_ref, shared_down_ref,
    expert_gate_ref, expert_up_ref, expert_down_ref, routes_ref, route_gate_ref,
    out_ref,
    weights, staged, eg, eu, ed, ag0, ag1, xn, token_block, slot_matrix,
    routes_all, gates_all, part, sib0, sib1, sums0, sums1, came0, came1, six, passed0, passed1,
    accum, slots_out, slots_in, hidden_acc, expert_out, expert_sib, back_out, back_in, part1,
    send_sem, recv_sem, local_sem,
):
    e = lax.axis_index("expert")
    t = lax.axis_index("tensor")
    y, x, zh = e // 8, lax.rem(e // 2, 4), lax.rem(e, 2)
    z = zh * 8 + t // 2
    c = lax.rem(t, 2)
    side = 1 - 2 * c
    other = 1 - zh
    oc = 1 - c

    def device(dy, dx, dz, dc):
        yy, xx = lax.rem(y + dy, 4), lax.rem(x + dx, 4)
        zz, cc = lax.rem(z + dz + 16, 16), lax.rem(c + dc, 2)
        return {"expert": (yy * 4 + xx) * 2 + zz // 8, "tensor": lax.rem(zz, 8) * 2 + cc}

    counter = [0]
    pending = []

    def send(src, dst, offset):
        k = counter[0]
        counter[0] += 1
        copy = pltpu.make_async_remote_copy(
            src_ref=src,
            dst_ref=dst,
            send_sem=send_sem.at[k],
            recv_sem=recv_sem.at[k],
            device_id=device(*offset),
            device_id_type=MESH,
        )
        copy.start()
        pending.append(copy)
        return copy

    def landed(copies):
        for copy in copies:
            copy.wait_recv()

    loads = [
        pltpu.make_async_copy(src.at[0], dst, local_sem.at[i])
        for i, (src, dst) in enumerate(
            ((expert_gate_ref, eg), (expert_up_ref, eu), (expert_down_ref, ed))
        )
    ]
    for load in loads:
        load.start()

    barrier = pltpu.get_barrier_semaphore()
    for offset in PARTNERS:
        pl.semaphore_signal(barrier, inc=1, device_id=device(*offset), device_id_type=MESH)

    dense_refs = (dense_gate_ref, dense_up_ref, dense_down_ref)
    shared_refs = (shared_gate_ref, shared_up_ref, shared_down_ref)
    mine = pl.multiple_of(zh * 256, 256)
    theirs = pl.multiple_of(other * 256, 256)
    for i, ref in enumerate(dense_refs):
        for h in range(2):
            weights[3 * h + i, y, x, zh] = ref[:, pl.ds(mine + 128 * h, 128)]
            staged[3 * h + i] = ref[:, pl.ds(theirs + 128 * h, 128)]
    mine = pl.multiple_of(zh * 128, 128)
    theirs = pl.multiple_of(other * 128, 128)
    for i, ref in enumerate(shared_refs):
        weights[6 + i, y, x, zh] = ref[:, pl.ds(mine, 128)]
        staged[6 + i] = ref[:, pl.ds(theirs, 128)]
    ag0[z, c] = tokens_ref[...]

    routes_all[zh] = jnp.broadcast_to(routes_ref[...], (8, TOK))
    gates_all[zh] = jnp.broadcast_to(route_gate_ref[...], (8, TOK))

    pl.semaphore_wait(barrier, len(PARTNERS))

    def plane_first(unit, half, x_first):
        lo, n = unit
        block = weights.at[pl.ds(lo, n), y, x, half]
        return [
            send(block, block, (0, d, 0, 0) if x_first else (d, 0, 0, 0)) for d in RING
        ]

    def plane_second(unit, half, x_first):
        lo, n = unit
        if x_first:
            block = weights.at[pl.ds(lo, n), y, :, half]
            return [send(block, block, (d, 0, 0, 0)) for d in RING]
        block = weights.at[pl.ds(lo, n), :, x, half]
        return [send(block, block, (0, d, 0, 0)) for d in RING]

    A, B, S = (0, 3), (3, 3), (6, 3)

    def spot(offset):
        return lax.rem(z + offset + 16, 16)

    def pass_on(buf, origin, steps, rows=slice(0, FEAT)):
        block = buf.at[spot(origin), c, rows]
        return [send(block, block, (0, 0, step, 0)) for step in steps]

    def pass_across(buf, origins):
        blocks = [buf.at[spot(origin), c] for origin in origins]
        return [send(block, block, (0, 0, 0, 1)) for block in blocks]

    def gather_start(buf):
        first = [pass_on(buf, 0, (3, -3), rows) for rows in HALVES]
        return first + [pass_on(buf, 0, (1, -1))], pass_across(buf, (0,))

    def gather_middle(buf, first, across):
        second = []
        for i, rows in enumerate(HALVES):
            landed(first[i][:1])
            forth = pass_on(buf, -3, (3,), rows)
            landed(first[i][1:])
            second.append(forth + pass_on(buf, 3, (-3,), rows))
        second.append(pass_on(buf, -3, (1, -1)) + pass_on(buf, 3, (-1, 1)))
        landed(first[2])
        across += pass_across(buf, (-3, 3, -1, 1))
        return second

    def gather_late(buf, second, across):
        third = []
        for i, rows in enumerate(HALVES):
            landed(second[i][:1])
            third += pass_on(buf, -6, (1, -1), rows)
            landed(second[i][1:])
            third += pass_on(buf, 6, (-1, 1), rows)
            third += pass_on(buf, -6 * side, (2 * side,), rows)
        landed(second[2])
        across += pass_across(buf, (-6, 6, -4, -2, 4, 2))
        return third

    def gather_end(buf, third, across):
        landed(third)
        across += pass_across(buf, (-7, -5, 7, 5, 8))
        landed(across)

    def plane_beside(unit, half, x_first):
        lo, n = unit
        if x_first:
            block = weights.at[pl.ds(lo, n), y, :, half]
            return [send(block, block, (d, 0, 0, 0)) for d in (1, 3)]
        block = weights.at[pl.ds(lo, n), :, x, half]
        return [send(block, block, (0, d, 0, 0)) for d in (1, 3)]

    def plane_beyond(unit, half, x_first, beside):
        lo, n = unit
        passed_on = []
        for copy, d, rows in zip(beside, (1, 3), (slice(0, 2), slice(2, 4))):
            landed([copy])
            if x_first:
                block = weights.at[pl.ds(lo, n), lax.rem(y + 4 - d, 4), rows, half]
                passed_on.append(send(block, block, (d, 0, 0, 0)))
            else:
                block = weights.at[pl.ds(lo, n), rows, lax.rem(x + 4 - d, 4), half]
                passed_on.append(send(block, block, (0, d, 0, 0)))
        return passed_on

    def cross_over(lo, n):
        block = weights.at[pl.ds(lo, n), y, x, zh]
        return [send(staged.at[pl.ds(lo, n)], block, (0, 0, 8, 0))]

    first, across = gather_start(ag0)
    own_a = plane_first(A, zh, True)
    own_b = plane_first(B, zh, False)
    order = (0, 1, 3, 4, 2, 5)
    cross = [cross_over(b, 1) for b in order]
    cross_meta = [
        send(routes_all.at[zh], routes_all.at[zh], (0, 0, 8, 0)),
        send(gates_all.at[zh], gates_all.at[zh], (0, 0, 8, 0)),
    ]
    part_1, part_2, part_3 = {}, {}, {}

    def crossed(i):
        landed(cross[i])
        part_1[i] = plane_first((order[i], 1), other, i % 2 == 0)

    def beside(i):
        landed(part_1[i])
        part_2[i] = plane_beside((order[i], 1), other, i % 2 == 0)

    def beyond(i):
        part_3[i] = plane_beyond((order[i], 1), other, i % 2 == 0, part_2[i])

    landed(own_a)
    own_a2 = plane_beside(A, zh, True)
    landed(own_b)
    own_b2 = plane_beside(B, zh, False)
    second = gather_middle(ag0, first, across)
    crossed(0)
    crossed(1)
    crossed(2)
    beside(0)
    crossed(3)
    beside(1)
    crossed(4)
    own_3 = plane_beyond(A, zh, True, own_a2) + plane_beyond(B, zh, False, own_b2)
    third = gather_late(ag0, second, across)
    cross_s = cross_over(6, 3)
    beside(2)
    crossed(5)
    beside(3)
    beyond(0)
    beside(4)
    beyond(1)
    beside(5)
    for i in range(2, 6):
        beyond(i)
    own_s = plane_first(S, zh, True)
    gather_end(ag0, third, across)

    landed(cross_meta)
    columns = []
    before = lax.broadcasted_iota(jnp.int32, (TOK, TOK), 0) < lax.broadcasted_iota(
        jnp.int32, (TOK, TOK), 1
    )
    for h in range(2):
        row = jnp.broadcast_to(routes_all[h][:1], (TOK, TOK))
        column = row.astype(F32).T.astype(jnp.int32)
        rank = jnp.sum(((row == column) & before).astype(F32), axis=0, keepdims=True)
        row = row[:1]
        slot = jnp.where((row & 1) == zh, (row >> 1) * 16 + h * DEPTH + rank.astype(jnp.int32), -1)
        columns.append(lax.broadcasted_iota(jnp.int32, (256, TOK), 0) == slot)
    slot_matrix[...] = jnp.concatenate(columns, axis=1).astype(F32).astype(BF16)

    def normalise(buf, gain_ref):
        eye = identity(TOK)
        squares = [jnp.zeros((TOK, 1), F32)] * 2
        for i in range(4):
            for h in range(2):
                block = buf[8 * h + 2 * i : 8 * h + 2 * i + 2].reshape(640, TOK)
                rows = dot(eye, block, NT)
                xn[h * TOK : (h + 1) * TOK, 640 * i : 640 * (i + 1)] = rows.astype(BF16)
                squares[h] = squares[h] + jnp.sum(rows * rows, axis=1, keepdims=True)
        for h in range(2):
            scale = lax.rsqrt(squares[h] * (1.0 / D) + EPSILON)
            for i in range(4):
                at = (slice(h * TOK, (h + 1) * TOK), slice(640 * i, 640 * (i + 1)))
                gain = gain_ref[640 * i : 640 * (i + 1)][None, :]
                xn[at] = (xn[at].astype(F32) * scale * gain).astype(BF16)

    normalise(ag0, first_gain_ref)

    landed(own_3 + part_3[0] + part_3[1] + part_3[2] + part_3[3])

    def columns_of(blocks, yy):
        return jnp.concatenate([weights[b, yy].reshape(640, 128) for b in blocks], axis=1)

    hidden = jnp.zeros((256, 512), F32)
    for yy in range(4):
        hidden += dot(xn[:, 640 * yy : 640 * (yy + 1)], columns_of((0, 3, 1, 4), yy), NN)
    hidden = gated(hidden[:, :256], hidden[:, 256:])
    landed(part_3[4] + part_3[5])
    for zlo in range(8):
        rows = jnp.concatenate(
            [weights[b, zlo // 2, 2 * (zlo % 2) : 2 * (zlo % 2) + 2].reshape(320, 128) for b in (2, 5)],
            axis=1,
        )
        terms = dot(rows, hidden, NT).astype(BF16)
        for h in range(2):
            part[8 * h + zlo] = terms[:, h * TOK : (h + 1) * TOK].reshape(2, FEAT, TOK)

    def reduce_scatter(part, sib, sums, came, six, passed, meanwhile):
        deep = (-7, -5, 7, 5, 8)
        middle = (-4, -2, 4, 2)
        rest = (-6, 6, -3, 3, -1, 1, 0)
        across = {
            o: send(part.at[spot(o), oc], sib.at[spot(o)], (0, 0, 0, 1)) for o in deep + middle + rest
        }

        def add_cores(o):
            landed([across[o]])
            i = spot(o)
            sums[i] = (part[i, c].astype(F32) + sib[i].astype(F32)).astype(BF16)

        slots = [0]

        def leave(o, step):
            slots[0] += 1
            slot = came.at[slots[0] - 1]
            return slots[0] - 1, send(sums.at[spot(o)], slot, (0, 0, step, 0))

        legs = {}
        for o, step in zip(deep, (-1, 1, 1, -1, -2 * side)):
            add_cores(o)
            legs[o] = leave(o, step)
        for o, step in zip(middle, (-1, 1, 1, -1)):
            add_cores(o)
            legs[o] = leave(o, step)
        for o in rest:
            add_cores(o)
            if o in (-1, 1):
                legs[o] = leave(o, o)
        def from_here(legs, rows):
            return sum(came[leg[0], rows].astype(F32) for leg in legs)

        landed([legs[o][1] for o in (-7, -5, 7, 5, 8)])
        for h, rows in enumerate(HALVES):
            six[0, rows] = sums[spot(-6), rows].astype(F32) + from_here((legs[-7], legs[-5]), rows)
            six[1, rows] = sums[spot(6), rows].astype(F32) + from_here((legs[7], legs[5]), rows)
            six[c, rows] += came[legs[8][0], rows].astype(F32)
            for i, o in enumerate((-6, 6)):
                passed[i, rows] = six[i, rows].astype(BF16)
                copy = send(passed.at[i, rows], came.at[11 + i, rows], (0, 0, o // 2, 0))
                legs[o, h] = (11 + i, copy)
        meanwhile()
        landed([legs[o][1] for o in (-4, -2, 4, 2)])
        for h, rows in enumerate(HALVES):
            for i, s in enumerate((-1, 1)):
                landed([legs[6 * s, h][1]])
                three = sums[spot(3 * s), rows].astype(F32)
                three += from_here((legs[2 * s], legs[4 * s], legs[6 * s, h]), rows)
                passed[2 + i, rows] = three.astype(BF16)
                copy = send(passed.at[2 + i, rows], came.at[13 + i, rows], (0, 0, 3 * s, 0))
                legs[3 * s, h] = (13 + i, copy)
        landed([legs[-1][1], legs[1][1]])
        landed([legs[3 * s, h][1] for s in (-1, 1) for h in range(2)])
        total = sums[z].astype(F32)
        for leg in (9, 10, 13, 14):
            total += came[leg].astype(F32)
        return total

    late = {}

    def shared_weights():
        landed(cross_s)
        late["part"] = plane_first(S, other, False)
        landed(own_s)
        late["own"] = plane_second(S, zh, True)

    middle = reduce_scatter(part, sib0, sums0, came0, six, passed0, shared_weights)
    middle = (tokens_ref[...].astype(F32) + middle).astype(BF16)
    token_block[...] = middle
    ag1[z, c] = middle
    first, across = gather_start(ag1)
    landed(late["part"])
    part_s2 = plane_second(S, other, False)
    second = gather_middle(ag1, first, across)
    third = gather_late(ag1, second, across)
    gather_end(ag1, third, across)
    normalise(ag1, second_gain_ref)

    half = pl.multiple_of(c * HALF, HALF)
    for i in range(5):
        piece = dot(slot_matrix[...], xn[:, pl.ds(half + 256 * i, 256)], NN)
        slots_out[:, 256 * i : 256 * (i + 1)] = piece.astype(BF16)

    def rows_of(yy, xx):
        return pl.ds(pl.multiple_of((yy * 4 + xx) * 16, 16), 16)

    own_rows = rows_of(y, x)

    def exchange(src, dst):
        return [
            send(
                src.at[rows_of(lax.rem(y + a, 4), lax.rem(x + b, 4))],
                dst.at[own_rows],
                (a, b, 0, 0),
            )
            for a, b in PLANE
        ]

    dispatched = exchange(slots_out, slots_in.at[c])
    slots_in[c, own_rows] = slots_out[own_rows]

    landed(late["own"] + part_s2)
    hidden = jnp.zeros((256, 256), F32)
    for yy in range(4):
        hidden += dot(xn[:, 640 * yy : 640 * (yy + 1)], columns_of((6, 7), yy), NN)
    hidden = gated(hidden[:, :128], hidden[:, 128:])
    for yy in range(4):
        accum[640 * yy : 640 * (yy + 1)] = dot(weights[8, yy].reshape(640, 128), hidden, NT)

    swapped = []
    for k, (a, b) in enumerate([(0, 0)] + PLANE):
        if k:
            landed(dispatched[k - 1 : k])
        block = slots_in.at[c, rows_of(lax.rem(y + 4 - a, 4), lax.rem(x + 4 - b, 4))]
        swapped.append(send(block, block, (0, 0, 0, 1)))
    for load in loads:
        load.wait()

    def expert_half(h):
        base = pl.multiple_of(h * HALF, HALF)
        rows = slots_in.at[h]
        for i in range(5):
            k = pl.ds(base + 256 * i, 256)
            piece = rows[:, 256 * i : 256 * (i + 1)]
            hidden_acc[:, :256] += dot(piece, eg[k, :], NN)
            hidden_acc[:, 256:] += dot(piece, eu[k, :], NN)

    hidden_acc[...] = jnp.zeros_like(hidden_acc)
    expert_half(c)
    landed(swapped)
    expert_half(oc)
    hidden = gated(hidden_acc[:, :256], hidden_acc[:, 256:])
    def expert_rows(h, i):
        k = pl.ds(pl.multiple_of(h * HALF, HALF) + 256 * i, 256)
        return dot(hidden, ed[k, :], NT)

    crossing = []
    for i in range(5):
        cols = slice(256 * i, 256 * (i + 1))
        expert_out[:, cols] = expert_rows(oc, i).astype(BF16)
        crossing.append(send(expert_out.at[:, cols], expert_sib.at[:, cols], (0, 0, 0, 1)))
    for i in range(5):
        cols = slice(256 * i, 256 * (i + 1))
        rows = expert_rows(c, i)
        landed(crossing[i : i + 1])
        back_out[:, cols] = (rows + expert_sib[:, cols].astype(F32)).astype(BF16)
    returned = exchange(back_out, back_in)
    back_in[own_rows] = back_out[own_rows]
    landed(returned)

    gates = jnp.concatenate([gates_all[0][:1], gates_all[1][:1]], axis=1)
    for i in range(5):
        routed = dot(back_in[:, 256 * i : 256 * (i + 1)], slot_matrix[...], TN)
        accum[pl.ds(half + 256 * i, 256)] += routed * gates
    for zlo in range(8):
        terms = accum[320 * zlo : 320 * (zlo + 1)].astype(BF16)
        for h in range(2):
            part1[8 * h + zlo] = terms[:, h * TOK : (h + 1) * TOK].reshape(2, FEAT, TOK)
    mixed = reduce_scatter(part1, sib1, sums1, came1, six, passed1, lambda: None)
    mixed = token_block[...].astype(F32) + mixed
    out_ref[...] = mixed.astype(BF16)
    assert counter[0] <= N_SEM
    for copy in pending:
        copy.wait_send()


def local(*args):
    args = list(args)
    args[0] = args[0].T
    args[12] = args[12].reshape(1, TOK)
    args[13] = args[13].reshape(1, TOK)
    vmem = pl.BlockSpec(memory_space=pltpu.VMEM)
    anywhere = pl.BlockSpec(memory_space=pl.ANY)
    ring = (16, FEAT, TOK)
    scratch = [
        ((9, 4, 4, 2, ROWS, 128), BF16),
        ((9, ROWS, 128), BF16),
        ((D, 256), BF16),
        ((D, 256), BF16),
        ((D, 256), BF16),
        ((16, 2, FEAT, TOK), BF16),
        ((16, 2, FEAT, TOK), BF16),
        ((256, D), BF16),
        ((FEAT, TOK), BF16),
        ((256, 256), BF16),
        ((2, 8, TOK), jnp.int32),
        ((2, 8, TOK), F32),
        ((16, 2, FEAT, TOK), BF16),
        (ring, BF16),
        (ring, BF16),
        (ring, BF16),
        (ring, BF16),
        ((15, FEAT, TOK), BF16),
        ((15, FEAT, TOK), BF16),
        ((2, FEAT, TOK), F32),
        ((4, FEAT, TOK), BF16),
        ((4, FEAT, TOK), BF16),
        ((D, 256), F32),
        ((256, HALF), BF16),
        ((2, 256, HALF), BF16),
        ((256, 512), F32),
        ((256, HALF), BF16),
        ((256, HALF), BF16),
        ((256, HALF), BF16),
        ((256, HALF), BF16),
        ((16, 2, FEAT, TOK), BF16),
    ]
    return pl.pallas_call(
        kernel,
        out_shape=jax.ShapeDtypeStruct((FEAT, TOK), BF16),
        in_specs=[anywhere if 9 <= i < 12 else vmem for i in range(14)],
        out_specs=vmem,
        scratch_shapes=[pltpu.VMEM(shape, dtype) for shape, dtype in scratch]
        + [
            pltpu.SemaphoreType.DMA((N_SEM,)),
            pltpu.SemaphoreType.DMA((N_SEM,)),
            pltpu.SemaphoreType.DMA((3,)),
        ],
        compiler_params=pltpu.CompilerParams(
            collective_id=0, has_side_effects=True, vmem_limit_bytes=56 * 2**20
        ),
    )(*args).T


def solution(mesh):
    placed = (
        P("expert", "tensor"),
        P(),
        P("expert", "tensor"),
        P("expert", "tensor"),
        P("expert", "tensor"),
        P(),
        P("expert", "tensor"),
        P("expert", "tensor"),
        P("expert", "tensor"),
        P("expert", None, "tensor"),
        P("expert", None, "tensor"),
        P("expert", None, "tensor"),
        P("expert", None),
        P("expert", None),
    )
    return jax.shard_map(
        local, mesh=mesh, in_specs=placed, out_specs=P("expert", "tensor"), check_vma=False
    )
```
